32 devices in a mesh: groups: 2 (over x), expert: 16 (over z, y, core).
Axes of the slice: x: 2, y: 2, z: 4, core: 2. Of those that a mesh axis runs over, the one named last changes fastest.
Arguments:
- tokens: bfloat16 [4096, 5120], P(('groups', 'expert')), parts along dimension 0, may hold values from -6 to 6
- expert_ids: int32 [4096, 1], P(('groups', 'expert')), parts along dimension 0, may hold values from 0 to 3, as said below
- slot_ids: int32 [4096, 1], P(('groups', 'expert')), parts along dimension 0, may hold values from 0 to 10, as said below
- route_weights: float32 [4096, 1], P(('groups', 'expert')), parts along dimension 0, may hold values from 0.2 to 1
- cotangent: bfloat16 [4096, 5120], P(('groups', 'expert')), parts along dimension 0, may hold values from -6 to 6
- gate_weight: bfloat16 [5120, 3072], P(None, 'expert'), may hold values from -0.078125 to 0.078125
- up_weight: bfloat16 [5120, 3072], P(None, 'expert'), may hold values from -0.078125 to 0.078125
- down_weight: bfloat16 [3072, 5120], P('expert'), may hold values from -0.21875 to 0.21875
- trained: int32 [4], P('groups'), parts along dimension 0, may hold values from 0 to 3, as said below
Outputs:
- layer_out: bfloat16 [4096, 5120], P(('groups', 'expert')), parts along dimension 0
- token_grad: bfloat16 [4096, 5120], P(('groups', 'expert')), parts along dimension 0
- down_grad: bfloat16 [6144, 5120], P(('groups', 'expert')), parts along dimension 0
The draws below stay inside these ranges and needn't reach their ends.
There are 2 independent parts, one for each index of `groups`. The reference program is written for one: setup_inputs(seed, part) draws one part's arguments, and reference() takes and returns one part's arrays. A program takes and returns all parts, laid end to end along the dimension named above; an argument that names none is the same for every part. Nothing has to cross between parts.
Inputs may be any that keep to these rules, and one draw needn't show every extreme that they name: `expert_ids`: a token's 1 ids are distinct; every expert is named by some token. `slot_ids`: for the tokens of one device, the kept assignments to one expert have slots 0, 1, 2 and so on in order of token and choice; a slot of 10 marks an assignment dropped for lack of capacity; on every device some expert fills all 10 slots. `trained`: distinct expert ids.
All inputs are finite; a program needn't handle non-finite values.
Results may differ from the reference program's by a relative error of at most 0.0065.
Values may be sent and summed in bfloat16 or wider, within the bound.
A program may use at most 128 MiB of HBM per device.

```python
import jax
import jax.numpy as jnp
from jax import lax

D = 5120
SLICES = 4
HID_DEV = 192
TOP = 1
EXPERT_SLOTS = 10
TOK_DEV = 128
ROUTED_EXPERTS = 4
HIDDEN_SIZE = 768
TOKENS = 2048
TRAINED = 2
N_EXPERT = 16


def route_table(key):
    key_pop, key_noise, key_hot = jax.random.split(key, 3)
    source_count = TOKENS // TOK_DEV
    popular_experts = jax.random.randint(key_pop, (ROUTED_EXPERTS,), 0, 4)
    random_jitter = jax.random.randint(key_noise, (TOKENS, ROUTED_EXPERTS), 0, 65536)
    hot_of_source = jax.random.randint(key_hot, (source_count,), 0, ROUTED_EXPERTS).astype(jnp.int32)
    token_pos = jnp.arange(TOKENS, dtype=jnp.int32)
    device_position = token_pos % TOK_DEV
    favored_expert = hot_of_source[token_pos // TOK_DEV]
    expert_row_index = jnp.arange(ROUTED_EXPERTS, dtype=jnp.int32)[None, :]
    covered_slots = (device_position[:, None] == expert_row_index) & (device_position < ROUTED_EXPERTS)[:, None]
    inside_surge = (device_position >= ROUTED_EXPERTS) & (device_position < ROUTED_EXPERTS + EXPERT_SLOTS + 1)
    forced_popular_expert = inside_surge[:, None] & (favored_expert[:, None] == expert_row_index)
    extra_score = (covered_slots | forced_popular_expert).astype(jnp.int32)
    router_logits = random_jitter + popular_experts[None, :] * 16384 + extra_score * 1048576
    router_logits = router_logits * ROUTED_EXPERTS + expert_row_index
    ranked_vals, chosen = lax.top_k(router_logits, TOP)
    chosen = chosen.astype(jnp.int32)
    onehot = (chosen[:, :, None] == jnp.arange(ROUTED_EXPERTS, dtype=jnp.int32)).astype(jnp.int32)
    onehot = onehot.reshape(source_count, TOK_DEV * TOP, ROUTED_EXPERTS)
    ranks = jnp.cumsum(onehot, axis=1) - 1
    slots = jnp.sum(ranks * onehot, axis=2).reshape(TOKENS, TOP)
    return (chosen, jnp.minimum(slots, EXPERT_SLOTS).astype(jnp.int32))


def draw_expert_ids(key, part):
    shared = route_table(key)
    return shared[0]


def draw_slot_ids(key, part):
    shared = route_table(key)
    return shared[1]


def draw_trained(key, part):
    key = jax.random.fold_in(key, 3)
    shuffled = jax.random.permutation(key, jnp.arange(ROUTED_EXPERTS, dtype=jnp.int32))
    return shuffled[:TRAINED].astype(jnp.int32)


def shard_levels(key, extent, cuts, least, top_value):
    level, own = 1.0, jax.random.fold_in(key, 6)
    for dim, parts in cuts:
        heights = jnp.exp(jax.random.uniform(jax.random.fold_in(own, dim), (parts,), jnp.float32, least / len(cuts), top_value / len(cuts)))
        level = level * jnp.repeat(heights, extent[dim] // parts).reshape([-1 if axis == dim else 1 for axis in range(len(extent))])
    return level


def noise(rng, dims, deviation, reach, pieces=(), kind=jnp.bfloat16):
    entries = jax.random.normal(rng, dims, jnp.float32) * deviation
    if len(pieces) > 0:
        entries = shard_levels(rng, dims, pieces, -0.22, 0.18) * entries
    return jnp.clip(entries, min=-reach, max=reach).astype(kind)


def setup_inputs(seed: int = 0, part: int = 0) -> dict:
    keys = jax.random.split(jax.random.key(seed), 10)
    part_keys = jax.random.split(jax.random.fold_in(keys[9], part), 10)
    tokens = noise(part_keys[0], (TOKENS, D), 1.0, 6.0, ((0, 16),))
    expert_ids = draw_expert_ids(jax.random.fold_in(jax.random.fold_in(keys[9], part), 71), part)
    slot_ids = draw_slot_ids(jax.random.fold_in(jax.random.fold_in(keys[9], part), 71), part)
    route_weights = jnp.clip(0.2 + 0.8 * jax.random.uniform(part_keys[3], (TOKENS, TOP), jnp.float32) ** shard_levels(part_keys[3], (TOKENS, TOP), ((0, 16),), -0.2, 0.2), 0.2, 1.0)
    cotangent = noise(part_keys[4], (TOKENS, D), 1.0, 6.0, ((0, 16),))
    gate_weight = noise(keys[5], (D, ROUTED_EXPERTS * HIDDEN_SIZE), D ** -0.5, 0.078125, ((1, 16),))
    up_weight = noise(keys[6], (D, ROUTED_EXPERTS * HIDDEN_SIZE), D ** -0.5, 0.078125, ((1, 16),))
    down_weight = noise(keys[7], (ROUTED_EXPERTS * HIDDEN_SIZE, D), HIDDEN_SIZE ** -0.5, 0.21875, ((0, 16),))
    trained = draw_trained(jax.random.fold_in(jax.random.fold_in(keys[9], part), 71), part)
    return {"tokens": tokens, "expert_ids": expert_ids, "slot_ids": slot_ids, "route_weights": route_weights, "cotangent": cotangent, "gate_weight": gate_weight, "up_weight": up_weight, "down_weight": down_weight, "trained": trained}


def by_expert(rows):
    return rows.reshape(N_EXPERT, ROUTED_EXPERTS, EXPERT_SLOTS, D).transpose(1, 0, 2, 3).reshape(ROUTED_EXPERTS, N_EXPERT * EXPERT_SLOTS, D)


def make_buffers(tokens, cotangent, slot_code, route_weights):
    slot_total = ROUTED_EXPERTS * EXPERT_SLOTS
    blocks = slot_code.reshape(N_EXPERT, TOK_DEV, TOP)
    onehot = blocks[..., None] == jnp.arange(slot_total, dtype=jnp.int32)
    placer = jnp.any(onehot, axis=2).astype(jnp.float32)
    weighting = jnp.sum(jnp.where(onehot, route_weights.reshape(N_EXPERT, TOK_DEV, TOP)[..., None], 0.0), axis=(1, 2))
    rows_x = jnp.einsum("nts,ntd->nsd", placer, tokens.reshape(N_EXPERT, TOK_DEV, D).astype(jnp.float32), precision=lax.Precision.HIGHEST)
    rows_g = jnp.einsum("nts,ntd->nsd", placer, cotangent.reshape(N_EXPERT, TOK_DEV, D).astype(jnp.float32), precision=lax.Precision.HIGHEST)
    dispatched = rows_x.astype(jnp.bfloat16)
    scaled = (rows_g * weighting[..., None]).astype(jnp.bfloat16)
    return by_expert(dispatched), by_expert(scaled)


def share_sum(shares):
    rounded = lax.optimization_barrier(shares.astype(jnp.bfloat16))
    return jnp.sum(rounded.astype(jnp.float32), axis=0).astype(jnp.bfloat16)


def one_expert(operands):
    inputs, grads_in, gate_w, up_w, down_w, is_trained = operands
    row_count = inputs.shape[0]
    gate_pre = jnp.dot(inputs, gate_w, preferred_element_type=jnp.float32)
    up_pre = jnp.dot(inputs, up_w, preferred_element_type=jnp.float32)
    sigmoid_v = jax.nn.sigmoid(gate_pre)
    silu_v = gate_pre * sigmoid_v
    activated = (silu_v * up_pre).astype(jnp.bfloat16)
    act_split = activated.reshape(row_count, SLICES, HID_DEV).astype(jnp.float32)
    down_split = down_w.reshape(SLICES, HID_DEV, D).astype(jnp.float32)
    out_shares = jnp.einsum("rsh,shd->srd", act_split, down_split, precision=lax.Precision.HIGHEST)
    expert_out = share_sum(out_shares)
    hidden_grad = lax.dot_general(grads_in, down_w, (((1,), (1,)), ((), ())), preferred_element_type=jnp.float32)
    up_grad = (hidden_grad * silu_v).astype(jnp.bfloat16)
    gate_grad = (hidden_grad * up_pre * sigmoid_v * (1.0 + gate_pre * (1.0 - sigmoid_v))).astype(jnp.bfloat16)
    gate_split = gate_w.reshape(D, SLICES, HID_DEV).astype(jnp.float32)
    up_split = up_w.reshape(D, SLICES, HID_DEV).astype(jnp.float32)
    gg_split = gate_grad.reshape(row_count, SLICES, HID_DEV).astype(jnp.float32)
    ug_split = up_grad.reshape(row_count, SLICES, HID_DEV).astype(jnp.float32)
    in_shares = jnp.einsum("rsh,dsh->srd", gg_split, gate_split, precision=lax.Precision.HIGHEST)
    in_shares = in_shares + jnp.einsum("rsh,dsh->srd", ug_split, up_split, precision=lax.Precision.HIGHEST)
    input_grad = share_sum(in_shares)
    product = lax.dot_general(activated, grads_in, (((0,), (0,)), ((), ())), preferred_element_type=jnp.float32)
    grad_rows = jnp.where(is_trained, product, 0.0).astype(jnp.bfloat16)
    return expert_out, input_grad, grad_rows


def combine(per_expert, slot_code, factor):
    source = per_expert.reshape(ROUTED_EXPERTS, N_EXPERT, EXPERT_SLOTS, D).transpose(1, 0, 2, 3).reshape(N_EXPERT * ROUTED_EXPERTS * EXPERT_SLOTS, D)
    blocks = slot_code.reshape(N_EXPERT, TOK_DEV * TOP)
    offset = jnp.arange(N_EXPERT, dtype=jnp.int32)[:, None] * (ROUTED_EXPERTS * EXPERT_SLOTS)
    rows_at = (jnp.maximum(blocks, 0) + offset).reshape(TOKENS, TOP).astype(jnp.int32)
    picked = source[rows_at].astype(jnp.float32)
    return jnp.sum(picked * factor[..., None], axis=1).astype(jnp.bfloat16)


def reference(tokens, expert_ids, slot_ids, route_weights, cotangent, gate_weight, up_weight, down_weight, trained):
    kept_mask = slot_ids < EXPERT_SLOTS
    slot_code = jnp.where(kept_mask, expert_ids * EXPERT_SLOTS + slot_ids, -1).astype(jnp.int32)
    inputs, grads_in = make_buffers(tokens, cotangent, slot_code, route_weights)
    gate_all = gate_weight.reshape(D, ROUTED_EXPERTS, HIDDEN_SIZE).transpose(1, 0, 2)
    up_all = up_weight.reshape(D, ROUTED_EXPERTS, HIDDEN_SIZE).transpose(1, 0, 2)
    down_all = down_weight.reshape(ROUTED_EXPERTS, HIDDEN_SIZE, D)
    flags = jnp.any(trained[None, :] == jnp.arange(ROUTED_EXPERTS, dtype=jnp.int32)[:, None], axis=1)
    expert_out, input_grad, grad_rows = lax.map(one_expert, (inputs, grads_in, gate_all, up_all, down_all, flags))
    layer_out = combine(expert_out, slot_code, jnp.where(kept_mask, route_weights, 0.0))
    token_grad = combine(input_grad, slot_code, kept_mask.astype(jnp.float32))
    return layer_out, token_grad, grad_rows.reshape(ROUTED_EXPERTS * HIDDEN_SIZE, D)
```

```python
import functools

import jax
import jax.numpy as jnp
from jax import lax
from jax.experimental import pallas as pl
from jax.experimental.pallas import tpu as pltpu
from jax.sharding import PartitionSpec as P

SLICES = 4
SLOTS = 10
FULL = 8
MESH = pl.DeviceIdType.MESH
F32 = jnp.float32
BF16 = jnp.bfloat16


def iota(shape, dim):
    return lax.broadcasted_iota(jnp.int32, shape, dim)


def dot(a, b, ca=1, cb=0):
    return lax.dot_general(a, b, (((ca,), (cb,)), ((), ())), preferred_element_type=F32)


def fold(low, high, blocks, b, tail):
    width = low.shape[1]
    split = blocks * 8

    def pair(lo, hi):
        lo = lo.reshape(blocks, 1, 8, width)
        hi = hi.reshape(blocks, 1, 8, width)
        return jnp.concatenate([lo, hi], axis=1).reshape(blocks, 16, width)

    main = pair(low[:split], high[:split]).astype(BF16)
    rest = pair(low[split:], high[split:])
    mine = ((iota((1, 16, 1), 1) & 7) >> 1) == b
    return main, jnp.where(mine, rest, tail)


def unfold(total, blocks):
    split = blocks * 16
    width = total.shape[1]
    main = total[:split].reshape(blocks, 2, 8, width)
    main = (main[:, 0] + main[:, 1]).reshape(blocks * 8, width)
    rest = total[split:].reshape(blocks, 2, 8, width)
    rest = rest[:, 0] + rest[:, 1]
    even = (iota((1, 8, 1), 1) & 1) == 0
    first = jnp.sum(jnp.where(even, rest, 0.0), axis=1, keepdims=True)
    second = jnp.sum(jnp.where(even, 0.0, rest), axis=1, keepdims=True)
    rest = jnp.where(even, first, second).reshape(blocks * 8, width)
    return jnp.concatenate([main, rest], axis=0)


def exchange_kernel(
    n,
    ids_ref,
    slots_ref,
    weights_ref,
    trained_ref,
    tokens_hbm,
    cot_hbm,
    gate_hbm,
    up_hbm,
    down_hbm,
    ret_ref,
    dgrad_ref,
    tokens,
    cot,
    gate,
    up,
    down,
    send,
    recv,
    total,
    hidden,
    act,
    wide,
    shares,
    cross,
    ysend,
    yrecv,
    load_sem,
    z_sem,
    y_sem,
    c_sem,
    recv_sem,
    own_sem,
    cs_sem,
    cr_sem,
    ys_sem,
    yr_sem,
    zs_sem,
    zr_sem,
):
    experts = n // SLICES
    model = tokens.shape[1]
    part = model // 8
    body = model // 2
    group = min(n, 16)
    groups = n // group
    me = lax.axis_index("expert")
    expert, low = me // 4, lax.rem(me, 4)
    core, side = lax.rem(me, 2), low // 2
    core_peer = me + 1 - 2 * core
    side_peer = me + 2 - 4 * side
    order = [k for k in range(experts) if k >= 2] + [1]

    def other(k):
        if experts & (experts - 1) == 0:
            step, out = 1, 0
            for bit in range(experts.bit_length() - 1):
                have = lax.rem(expert // step, 2)
                out = out + step * (1 - have if k & step else have)
                step *= 2
            return out
        return lax.rem(expert + k, experts)

    def back(k):
        if experts & (experts - 1) == 0:
            return other(k)
        return lax.rem(expert + experts - k, experts)

    def remote(src, dst, ssem, rsem, dev):
        return pltpu.make_async_remote_copy(
            src_ref=src,
            dst_ref=dst,
            send_sem=ssem,
            recv_sem=rsem,
            device_id={"expert": dev},
            device_id_type=MESH,
        )

    loads = [
        pltpu.make_async_copy(s, d, load_sem.at[i])
        for i, (s, d) in enumerate(
            [
                (tokens_hbm, tokens),
                (cot_hbm, cot),
                (gate_hbm, gate),
                (up_hbm, up),
                (down_hbm, down),
            ]
        )
    ]
    for copy in loads:
        copy.start()

    barrier = pltpu.get_barrier_semaphore()
    for k in range(1, experts):
        pl.semaphore_signal(
            barrier, inc=1, device_id={"expert": other(k) * 4 + low}, device_id_type=MESH
        )
    for dev in (core_peer, side_peer):
        pl.semaphore_signal(barrier, inc=1, device_id={"expert": dev}, device_id_type=MESH)

    rows = experts * 16
    row = iota((rows, 1), 0)
    half = experts * 8
    want = jnp.where(
        row < half,
        (row >> 3) * SLOTS + (row & 7),
        ((row - half) >> 3) * SLOTS + FULL + (row & 1),
    )
    placer = jnp.zeros((rows, tokens.shape[0]), F32)
    factor = jnp.zeros((rows, 1), F32)
    for k in range(ids_ref.shape[0]):
        slot = slots_ref[k : k + 1, :]
        code = jnp.where(slot < SLOTS, ids_ref[k : k + 1, :] * SLOTS + slot, -1)
        hit = code == want
        placer = jnp.where(hit, 1.0, placer)
        factor = factor + jnp.sum(
            jnp.where(hit, weights_ref[k : k + 1, :], 0.0), axis=1, keepdims=True
        )
    placer = placer.astype(BF16)

    z_copies, y_copies, c_copies, own = {}, {}, {}, []
    for a, source in enumerate((tokens, cot)):
        loads[a].wait()
        tail = jnp.zeros((experts, 16, part), F32)
        for b in range(4):
            lo = dot(placer, source[:, b * part : (b + 1) * part])
            hi = dot(placer, source[:, (b + 4) * part : (b + 5) * part])
            if a == 1:
                lo, hi = lo * factor, hi * factor
            main, tail = fold(lo, hi, experts, b, tail)
            send[a, :, :, b * part : (b + 1) * part] = main
        send[a, :, :, body:] = tail.astype(BF16)
        if a == 0:
            pl.semaphore_wait(barrier, experts + 1)
        for k in order:
            target = other(k)
            copy = remote(
                send.at[a, target],
                recv.at[a, me],
                z_sem.at[a, k],
                recv_sem.at[a, me],
                target * 4 + low,
            )
            copy.start()
            z_copies[a, k] = copy
        mine = send.at[a, expert]
        for book, sem, dev in ((y_copies, y_sem, side_peer), (c_copies, c_sem, core_peer)):
            copy = remote(mine, recv.at[a, me], sem.at[a, 0], recv_sem.at[a, me], dev)
            copy.start()
            book[a, 0] = copy
        copy = pltpu.make_async_copy(mine, recv.at[a, me], own_sem.at[a])
        copy.start()
        own.append(copy)

    def arrived(a, j):
        view = recv.at[a, j]
        remote(view, view, z_sem.at[a, 0], recv_sem.at[a, j], core_peer).wait_recv()

    def forward(a):
        def pass_side(k):
            j = back(k) * 4 + low + 2 - 4 * side
            arrived(a, j)
            view = recv.at[a, j]
            copy = remote(
                view, view, c_sem.at[a, experts + k], recv_sem.at[a, j], core_peer
            )
            copy.start()
            c_copies[a, experts + k] = copy

        before = 0
        for k in order:
            j = back(k) * 4 + low
            arrived(a, j)
            view = recv.at[a, j]
            copy = remote(view, view, y_sem.at[a, k], recv_sem.at[a, j], side_peer)
            copy.start()
            y_copies[a, k] = copy
            copy = remote(view, view, c_sem.at[a, k], recv_sem.at[a, j], core_peer)
            copy.start()
            c_copies[a, k] = copy
            pass_side(before)
            before = k
        pass_side(before)
        for k in [0] + order:
            for other_side in (0, 1):
                j = back(k) * 4 + 2 * (side if other_side == 0 else 1 - side) + 1 - core
                arrived(a, j)
        own[a].wait()

    trow = iota((2 * group * 16, 1), 0)
    packed_row = jnp.where(trow < group * 16, (trow >> 3) & 1, (trow & 15) >> 1)

    def eighth(q):
        return pl.ds(pl.multiple_of(q * part, 128), part)

    def packed(a, g, q):
        at = pl.ds(g * group, group)
        main = recv[a, at, :, pl.ds(pl.multiple_of(lax.rem(q, 4) * part, 128), part)]
        rest = recv[a, at, :, body:]
        both = jnp.concatenate([main, rest], axis=0)
        return both.reshape(2 * group * 16, part)

    def picked(q):
        return packed_row == jnp.where(trow < group * 16, q // 4, q)

    def over_groups(step):
        if groups == 1:
            step(0)
        else:
            lax.fori_loop(0, groups, lambda g, c: (step(g), c)[1], 0)

    def project(g, a, products):
        for i in range(len(products)):
            total[i] = jnp.zeros(total.shape[1:], F32)

        def step(q, carry):
            left = packed(a, g, q)
            keep = picked(q)
            for i, product in enumerate(products):
                total[i] += jnp.where(keep, product(left, q), 0.0)
            return carry

        lax.fori_loop(0, 8, step, 0)
        return [unfold(total[i], group) for i in range(len(products))]

    def emit(g, a, product):
        tail = jnp.zeros((group, 16, part), F32)

        def put(value, columns):
            value = value.reshape(group // 2, 2, 16, part)
            at = pl.ds(g * (group // 2), group // 2)
            for parity in (0, 1):
                shares[a, parity, at, :, columns] = value[:, parity]

        for b in range(4):
            main, tail = fold(product(b), product(b + 4), group, b, tail)
            put(main, slice(b * part, (b + 1) * part))
        put(tail.astype(BF16), slice(body, body + part))

    cross_copies, yshare_copies, zshare_copies = [], {}, []

    def start_cross(a):
        for k in order + [0]:
            e = other(k)
            copy = remote(
                shares.at[a, 1 - core, pl.ds(2 * e, 2)],
                cross.at[a, pl.ds(2 * e, 2)],
                cs_sem.at[a, e],
                cr_sem.at[a, e],
                core_peer,
            )
            copy.start()
            cross_copies.append(copy)

    def start_side(a):
        for k in order + [0]:
            e = other(k)
            view = cross.at[a, pl.ds(2 * e, 2)]
            remote(view, view, cs_sem.at[a, e], cr_sem.at[a, e], core_peer).wait_recv()
            at = 2 * e + 1 - side
            ysend[a, e] = (
                shares[a, core, at].astype(F32) + cross[a, at].astype(F32)
            ).astype(BF16)
            copy = remote(
                ysend.at[a, e], yrecv.at[a, e], ys_sem.at[a, e], yr_sem.at[a, e], side_peer
            )
            copy.start()
            yshare_copies[a, k] = copy

    def start_home(a):
        for k in order + [0]:
            e = other(k)
            view = yrecv.at[a, e]
            remote(view, view, ys_sem.at[a, e], yr_sem.at[a, e], side_peer).wait_recv()
            at = 2 * e + side
            send[a, e] = (
                (shares[a, core, at].astype(F32) + cross[a, at].astype(F32))
                + yrecv[a, e].astype(F32)
            ).astype(BF16)
            if k == 0:
                copy = pltpu.make_async_copy(send.at[a, e], ret_ref.at[a, e], own_sem.at[a])
            else:
                copy = remote(
                    send.at[a, e],
                    ret_ref.at[a, expert],
                    zs_sem.at[a, k],
                    zr_sem.at[a, expert],
                    e * 4 + low,
                )
            copy.start()
            zshare_copies.append((k, copy))

    forward(0)
    loads[2].wait()
    loads[3].wait()
    loads[4].wait()

    def first(g):
        gate_pre, up_pre = project(
            g,
            0,
            [
                lambda left, q: dot(left, gate[:, eighth(q)], 1, 1),
                lambda left, q: dot(left, up[:, eighth(q)], 1, 1),
            ],
        )
        hidden[0, g] = gate_pre
        hidden[1, g] = up_pre
        active = (gate_pre * jax.nn.sigmoid(gate_pre) * up_pre).astype(BF16)
        act[0, g] = active
        emit(g, 0, lambda q: dot(active, down[:, q * part : (q + 1) * part]))

    over_groups(first)
    start_cross(0)
    forward(1)
    for book in (z_copies, y_copies, c_copies):
        for copy in book.values():
            copy.wait_send()
    start_side(0)

    def second(g):
        (hid,) = project(g, 1, [lambda left, q: dot(left, down[:, eighth(q)], 1, 1)])
        gate_pre, up_pre = hidden[0, g], hidden[1, g]
        sig = jax.nn.sigmoid(gate_pre)
        up_grad = (hid * (gate_pre * sig)).astype(BF16)
        gate_grad = (hid * up_pre * sig * (1.0 + gate_pre * (1.0 - sig))).astype(BF16)

        def product(q):
            columns = slice(q * part, (q + 1) * part)
            return dot(gate_grad, gate[:, columns]) + dot(up_grad, up[:, columns])

        emit(g, 1, product)

    over_groups(second)
    start_cross(1)
    start_home(0)
    start_side(1)

    def spread(g):
        active = act[0, g].astype(F32)
        parts = []
        for piece in (active[: group * 8], active[group * 8 :]):
            piece = piece.reshape(group, 1, 8, -1)
            parts.append(jnp.concatenate([piece, piece], axis=1).reshape(group * 16, -1))
        wide[g] = jnp.concatenate(parts, axis=0).T

    over_groups(spread)
    start_home(1)
    lane = iota((1, 2 * group * 16), 1)
    packed_lane = jnp.where(lane < group * 16, (lane >> 3) & 1, (lane & 15) >> 1)
    is_trained = trained_ref[0] == expert
    for i in range(1, trained_ref.shape[0]):
        is_trained = jnp.logical_or(is_trained, trained_ref[i] == expert)

    def weight_step(q, carry):
        keep = packed_lane == jnp.where(lane < group * 16, q // 4, q)

        def term(g):
            left = jnp.where(keep, wide[g], 0.0).astype(BF16)
            return dot(left, packed(1, g, q))

        if groups == 1:
            product = term(0)
        else:
            product = lax.fori_loop(
                1, groups, lambda g, c: c + term(g), term(0)
            )
        dgrad_ref[:, eighth(q)] = jnp.where(is_trained, product, 0.0).astype(BF16)
        return carry

    lax.fori_loop(0, 8, weight_step, 0)

    for copy in cross_copies:
        copy.wait_send()
    for copy in yshare_copies.values():
        copy.wait_send()
    for k, copy in zshare_copies:
        if k == 0:
            copy.wait()
        else:
            copy.wait_send()
    for a in (0, 1):
        for k in order:
            e = back(k)
            view = ret_ref.at[a, e]
            remote(view, view, zs_sem.at[a, 0], zr_sem.at[a, e], core_peer).wait_recv()


def combine_kernel(
    ids_ref, slots_ref, weights_ref, main_out, tail_out, main_in, tail_in, layer_ref, grad_ref
):
    q = pl.program_id(0)
    rows = main_out.shape[1] * 16
    row = iota((rows, 1), 0)
    base = (row >> 4) * SLOTS
    want_main = jnp.where(((row >> 3) & 1) == q // 4, base + (row & 7), -2)
    want_tail = jnp.where(((row & 15) >> 1) == q, base + FULL + (row & 1), -2)
    layer = grad = None
    for k in range(ids_ref.shape[0]):
        slot = slots_ref[k : k + 1, :]
        code = jnp.where(slot < SLOTS, ids_ref[k : k + 1, :] * SLOTS + slot, -1)
        left_main = (code == want_main).astype(F32).astype(BF16)
        left_tail = (code == want_tail).astype(F32).astype(BF16)

        def gathered(main, tail):
            width = main.shape[-1]
            return dot(left_main, main[0].reshape(rows, width), 0, 0) + dot(
                left_tail, tail[0].reshape(rows, width), 0, 0
            )

        out = gathered(main_out, tail_out) * weights_ref[:, k : k + 1]
        back = gathered(main_in, tail_in)
        layer = out if layer is None else layer + out
        grad = back if grad is None else grad + back
    layer_ref[...] = layer.astype(BF16)
    grad_ref[...] = grad.astype(BF16)


def local(
    n,
    tokens,
    expert_ids,
    slot_ids,
    route_weights,
    cotangent,
    gate_weight,
    up_weight,
    down_weight,
    trained,
):
    experts = n // SLICES
    count, model = tokens.shape
    hid = gate_weight.shape[1]
    part = model // 8
    packed = model * SLOTS // 16
    group = min(n, 16)
    groups = n // group
    ids, slots, weights = expert_ids.T, slot_ids.T, route_weights.T
    vmem = pl.BlockSpec(memory_space=pltpu.VMEM)
    anywhere = pl.BlockSpec(memory_space=pl.ANY)
    dma = pltpu.SemaphoreType.DMA
    returned, down_grad = pl.pallas_call(
        functools.partial(exchange_kernel, n),
        out_shape=(
            jax.ShapeDtypeStruct((2, experts, 16, packed), BF16),
            jax.ShapeDtypeStruct((hid, model), BF16),
        ),
        in_specs=[vmem] * 3 + [pl.BlockSpec(memory_space=pltpu.SMEM)] + [anywhere] * 5,
        out_specs=(anywhere, vmem),
        scratch_shapes=[
            pltpu.VMEM((count, model), BF16),
            pltpu.VMEM((count, model), BF16),
            pltpu.VMEM((hid, model), BF16),
            pltpu.VMEM((hid, model), BF16),
            pltpu.VMEM((hid, model), BF16),
            pltpu.VMEM((2, experts, 16, packed), BF16),
            pltpu.VMEM((2, n, 16, packed), BF16),
            pltpu.VMEM((2, group * 32, hid), F32),
            pltpu.VMEM((2, groups, group * 16, hid), F32),
            pltpu.VMEM((1, groups, group * 16, hid), BF16),
            pltpu.VMEM((groups, hid, group * 32), F32),
            pltpu.VMEM((2, 2, n // 2, 16, packed), BF16),
            pltpu.VMEM((2, n // 2, 16, packed), BF16),
            pltpu.VMEM((2, experts, 16, packed), BF16),
            pltpu.VMEM((2, experts, 16, packed), BF16),
            dma((5,)),
            dma((2, experts)),
            dma((2, experts)),
            dma((2, 2 * experts)),
            dma((2, n)),
            dma((2,)),
            dma((2, experts)),
            dma((2, experts)),
            dma((2, experts)),
            dma((2, experts)),
            dma((2, experts)),
            dma((2, experts)),
        ],
        compiler_params=pltpu.CompilerParams(
            collective_id=0, has_side_effects=True, vmem_limit_bytes=62 * 2**20
        ),
        name="exchange",
    )(ids, slots, weights, trained, tokens, cotangent, gate_weight.T, up_weight.T, down_weight)

    def piece(a, tail):
        return pl.BlockSpec(
            (1, experts, 16, part), lambda q: (a, 0, 0, 4 if tail else q % 4)
        )

    small = pl.BlockSpec((ids.shape[0], count), lambda q: (0, 0))
    layer_out, token_grad = pl.pallas_call(
        combine_kernel,
        grid=(8,),
        out_shape=(
            jax.ShapeDtypeStruct((count, model), BF16),
            jax.ShapeDtypeStruct((count, model), BF16),
        ),
        in_specs=[
            small,
            small,
            pl.BlockSpec((count, ids.shape[0]), lambda q: (0, 0)),
            piece(0, False),
            piece(0, True),
            piece(1, False),
            piece(1, True),
        ],
        out_specs=(
            pl.BlockSpec((count, part), lambda q: (0, q)),
            pl.BlockSpec((count, part), lambda q: (0, q)),
        ),
        name="combine",
    )(ids, slots, route_weights, returned, returned, returned, returned)
    return (layer_out, token_grad, down_grad)


def solution(mesh):
    spread = P(("groups", "expert"), None)
    placed = (
        spread,
        spread,
        spread,
        spread,
        spread,
        P(None, "expert"),
        P(None, "expert"),
        P("expert", None),
        P("groups"),
    )
    return jax.shard_map(
        functools.partial(local, mesh.shape["expert"]),
        mesh=mesh,
        in_specs=placed,
        out_specs=(spread, spread, spread),
        check_vma=False,
    )
```

```python
import functools

import jax
import jax.numpy as jnp
from jax import lax
from jax.experimental import pallas as pl
from jax.experimental.pallas import tpu as pltpu
from jax.sharding import PartitionSpec as P

SLICES = 4
SLOTS = 10
FULL = 8
WINDOW = 2
MESH = pl.DeviceIdType.MESH
F32 = jnp.float32
BF16 = jnp.bfloat16


def iota(shape, dim):
    return lax.broadcasted_iota(jnp.int32, shape, dim)


def dot(a, b, ca=1, cb=0):
    return lax.dot_general(a, b, (((ca,), (cb,)), ((), ())), preferred_element_type=F32)


def fold(low, high, blocks, b, tail):
    width = low.shape[1]
    split = blocks * 8

    def pair(lo, hi):
        lo = lo.reshape(blocks, 1, 8, width)
        hi = hi.reshape(blocks, 1, 8, width)
        return jnp.concatenate([lo, hi], axis=1).reshape(blocks, 16, width)

    main = pair(low[:split], high[:split]).astype(BF16)
    rest = pair(low[split:], high[split:])
    mine = ((iota((1, 16, 1), 1) & 7) >> 1) == b
    return main, jnp.where(mine, rest, tail)


def unfold(total, blocks):
    split = blocks * 16
    width = total.shape[1]
    main = total[:split].reshape(blocks, 2, 8, width)
    main = (main[:, 0] + main[:, 1]).reshape(blocks * 8, width)
    rest = total[split:].reshape(blocks, 2, 8, width)
    rest = rest[:, 0] + rest[:, 1]
    even = (iota((1, 8, 1), 1) & 1) == 0
    first = jnp.sum(jnp.where(even, rest, 0.0), axis=1, keepdims=True)
    second = jnp.sum(jnp.where(even, 0.0, rest), axis=1, keepdims=True)
    rest = jnp.where(even, first, second).reshape(blocks * 8, width)
    return jnp.concatenate([main, rest], axis=0)


def exchange_kernel(
    n,
    ids_ref,
    slots_ref,
    weights_ref,
    trained_ref,
    tokens_hbm,
    cot_hbm,
    gate_hbm,
    up_hbm,
    down_hbm,
    ret_ref,
    layer_hbm,
    dgrad_hbm,
    tokens,
    cot,
    gate,
    up,
    down,
    send,
    recv,
    total,
    hidden,
    act,
    wide,
    shares,
    cross,
    ysend,
    yrecv,
    home,
    layer,
    dgrad,
    load_sem,
    z_sem,
    y_sem,
    c_sem,
    recv_sem,
    own_sem,
    cs_sem,
    cr_sem,
    ys_sem,
    yr_sem,
    zs_sem,
    zr_sem,
    out_sem,
):
    experts = n // SLICES
    model = tokens.shape[1]
    part = model // 8
    body = model // 2
    group = min(n, 16)
    groups = n // group
    me = lax.axis_index("expert")
    expert, low = me // 4, lax.rem(me, 4)
    core, side = lax.rem(me, 2), low // 2
    core_peer = me + 1 - 2 * core
    side_peer = me + 2 - 4 * side
    order = list(range(1, experts))
    homeward = order[1:] + order[:1] + [0]
    rets = (home, ret_ref)

    def other(k):
        if experts & (experts - 1) == 0:
            step, out = 1, 0
            for bit in range(experts.bit_length() - 1):
                have = lax.rem(expert // step, 2)
                out = out + step * (1 - have if k & step else have)
                step *= 2
            return out
        return lax.rem(expert + k, experts)

    def back(k):
        if experts & (experts - 1) == 0:
            return other(k)
        return lax.rem(expert + experts - k, experts)

    def remote(src, dst, ssem, rsem, dev):
        return pltpu.make_async_remote_copy(
            src_ref=src,
            dst_ref=dst,
            send_sem=ssem,
            recv_sem=rsem,
            device_id={"expert": dev},
            device_id_type=MESH,
        )

    loads = [
        pltpu.make_async_copy(s, d, load_sem.at[i])
        for i, (s, d) in enumerate(
            [
                (tokens_hbm, tokens),
                (cot_hbm, cot),
                (gate_hbm, gate),
                (up_hbm, up),
                (down_hbm, down),
            ]
        )
    ]
    for copy in loads:
        copy.start()

    barrier = pltpu.get_barrier_semaphore()
    for k in range(1, experts):
        pl.semaphore_signal(
            barrier, inc=1, device_id={"expert": other(k) * 4 + low}, device_id_type=MESH
        )
    for dev in (core_peer, side_peer):
        pl.semaphore_signal(barrier, inc=1, device_id={"expert": dev}, device_id_type=MESH)

    rows = experts * 16
    row = iota((rows, 1), 0)
    half = experts * 8
    want = jnp.where(
        row < half,
        (row >> 3) * SLOTS + (row & 7),
        ((row - half) >> 3) * SLOTS + FULL + (row & 1),
    )
    placer = jnp.zeros((rows, tokens.shape[0]), F32)
    factor = jnp.zeros((rows, 1), F32)
    for k in range(ids_ref.shape[0]):
        slot = slots_ref[k : k + 1, :]
        code = jnp.where(slot < SLOTS, ids_ref[k : k + 1, :] * SLOTS + slot, -1)
        hit = code == want
        placer = jnp.where(hit, 1.0, placer)
        factor = factor + jnp.sum(
            jnp.where(hit, weights_ref[k : k + 1, :], 0.0), axis=1, keepdims=True
        )
    placer = placer.astype(BF16)

    z_copies, y_copies, c_copies, own = {}, {}, {}, []
    steps = [(a, k) for a in (0, 1) for k in order]

    def start_z(a, k):
        target = other(k)
        copy = remote(
            send.at[a, target],
            recv.at[a, me],
            z_sem.at[a, k],
            recv_sem.at[a, me],
            target * 4 + low,
        )
        copy.start()
        z_copies[a, k] = copy

    for a, source in enumerate((tokens, cot)):
        loads[a].wait()
        tail = jnp.zeros((experts, 16, part), F32)
        for b in range(4):
            lo = dot(placer, source[:, b * part : (b + 1) * part])
            hi = dot(placer, source[:, (b + 4) * part : (b + 5) * part])
            if a == 1:
                lo, hi = lo * factor, hi * factor
            main, tail = fold(lo, hi, experts, b, tail)
            send[a, :, :, b * part : (b + 1) * part] = main
        send[a, :, :, body:] = tail.astype(BF16)
        if a == 0:
            pl.semaphore_wait(barrier, experts + 1)
            for pair in steps[:WINDOW]:
                start_z(*pair)
        mine = send.at[a, expert]
        for book, sem, dev in ((y_copies, y_sem, side_peer), (c_copies, c_sem, core_peer)):
            copy = remote(mine, recv.at[a, me], sem.at[a, 0], recv_sem.at[a, me], dev)
            copy.start()
            book[a, 0] = copy
        copy = pltpu.make_async_copy(mine, recv.at[a, me], own_sem.at[a])
        copy.start()
        own.append(copy)

    def arrived(a, j):
        view = recv.at[a, j]
        remote(view, view, z_sem.at[a, 0], recv_sem.at[a, j], core_peer).wait_recv()

    def pass_side(a, k):
        j = back(k) * 4 + low + 2 - 4 * side
        arrived(a, j)
        view = recv.at[a, j]
        copy = remote(view, view, c_sem.at[a, experts + k], recv_sem.at[a, j], core_peer)
        copy.start()
        c_copies[a, experts + k] = copy

    def pass_step(at):
        a, k = steps[at]
        j = back(k) * 4 + low
        arrived(a, j)
        if at + WINDOW < len(steps):
            start_z(*steps[at + WINDOW])
        view = recv.at[a, j]
        for book, sem, dev in ((y_copies, y_sem, side_peer), (c_copies, c_sem, core_peer)):
            copy = remote(view, view, sem.at[a, k], recv_sem.at[a, j], dev)
            copy.start()
            book[a, k] = copy

    def gathered(a):
        for k in [0] + order:
            for other_side in (0, 1):
                j = back(k) * 4 + 2 * (side if other_side == 0 else 1 - side) + 1 - core
                arrived(a, j)
        own[a].wait()

    trow = iota((2 * group * 16, 1), 0)
    packed_row = jnp.where(trow < group * 16, (trow >> 3) & 1, (trow & 15) >> 1)

    def eighth(q):
        return pl.ds(pl.multiple_of(q * part, 128), part)

    def packed(a, g, q):
        at = pl.ds(g * group, group)
        main = recv[a, at, :, pl.ds(pl.multiple_of(lax.rem(q, 4) * part, 128), part)]
        rest = recv[a, at, :, body:]
        both = jnp.concatenate([main, rest], axis=0)
        return both.reshape(2 * group * 16, part)

    def picked(q):
        return packed_row == jnp.where(trow < group * 16, q // 4, q)

    def over_groups(step):
        if groups == 1:
            step(0)
        else:
            lax.fori_loop(0, groups, lambda g, c: (step(g), c)[1], 0)

    def project(g, a, products):
        for i in range(len(products)):
            total[i] = jnp.zeros(total.shape[1:], F32)

        def step(q, carry):
            left = packed(a, g, q)
            keep = picked(q)
            for i, product in enumerate(products):
                total[i] += jnp.where(keep, product(left, q), 0.0)
            return carry

        lax.fori_loop(0, 8, step, 0)
        return [unfold(total[i], group) for i in range(len(products))]

    def emit(g, a, product):
        tail = jnp.zeros((group, 16, part), F32)

        def put(value, columns):
            value = value.reshape(group // 2, 2, 16, part)
            at = pl.ds(g * (group // 2), group // 2)
            for parity in (0, 1):
                shares[a, parity, at, :, columns] = value[:, parity]

        for b in range(4):
            main, tail = fold(product(b), product(b + 4), group, b, tail)
            put(main, slice(b * part, (b + 1) * part))
        put(tail.astype(BF16), slice(body, body + part))

    cross_copies, yshare_copies, zshare_copies = [], {}, []

    def start_cross(a):
        for k in homeward:
            e = other(k)
            copy = remote(
                shares.at[a, 1 - core, pl.ds(2 * e, 2)],
                cross.at[a, pl.ds(2 * e, 2)],
                cs_sem.at[a, e],
                cr_sem.at[a, e],
                core_peer,
            )
            copy.start()
            cross_copies.append(copy)

    def start_side(a):
        for k in homeward:
            e = other(k)
            view = cross.at[a, pl.ds(2 * e, 2)]
            remote(view, view, cs_sem.at[a, e], cr_sem.at[a, e], core_peer).wait_recv()
            at = 2 * e + 1 - side
            ysend[a, e] = (
                shares[a, core, at].astype(F32) + cross[a, at].astype(F32)
            ).astype(BF16)
            copy = remote(
                ysend.at[a, e], yrecv.at[a, e], ys_sem.at[a, e], yr_sem.at[a, e], side_peer
            )
            copy.start()
            yshare_copies[a, k] = copy

    def start_home(a, between=()):
        for turn, k in enumerate(homeward):
            e = other(k)
            view = yrecv.at[a, e]
            remote(view, view, ys_sem.at[a, e], yr_sem.at[a, e], side_peer).wait_recv()
            at = 2 * e + side
            send[a, e] = (
                (shares[a, core, at].astype(F32) + cross[a, at].astype(F32))
                + yrecv[a, e].astype(F32)
            ).astype(BF16)
            if k == 0:
                copy = pltpu.make_async_copy(send.at[a, e], rets[a].at[e], own_sem.at[a])
            else:
                copy = remote(
                    send.at[a, e],
                    rets[a].at[expert],
                    zs_sem.at[a, k],
                    zr_sem.at[a, expert],
                    e * 4 + low,
                )
            copy.start()
            zshare_copies.append((a, k, copy))
            if turn < len(between):
                between[turn]()

    last = len(order)
    for at in range(last):
        pass_step(at)
        pass_side(0, at)
    pass_step(last)
    pass_side(0, last)
    gathered(0)
    loads[2].wait()
    loads[3].wait()
    loads[4].wait()

    def first(g):
        gate_pre, up_pre = project(
            g,
            0,
            [
                lambda left, q: dot(left, gate[:, eighth(q)], 1, 1),
                lambda left, q: dot(left, up[:, eighth(q)], 1, 1),
            ],
        )
        hidden[0, g] = gate_pre
        hidden[1, g] = up_pre
        active = (gate_pre * jax.nn.sigmoid(gate_pre) * up_pre).astype(BF16)
        act[0, g] = active
        emit(g, 0, lambda q: dot(active, down[:, q * part : (q + 1) * part]))

    over_groups(first)
    start_cross(0)
    for at in range(last + 1, 2 * last):
        pass_side(1, at - last - 1)
        pass_step(at)
    pass_side(1, last - 1)
    pass_side(1, last)
    gathered(1)
    for book in (z_copies, y_copies, c_copies):
        for copy in book.values():
            copy.wait_send()
    start_side(0)

    def second(g):
        (hid,) = project(g, 1, [lambda left, q: dot(left, down[:, eighth(q)], 1, 1)])
        gate_pre, up_pre = hidden[0, g], hidden[1, g]
        sig = jax.nn.sigmoid(gate_pre)
        up_grad = (hid * (gate_pre * sig)).astype(BF16)
        gate_grad = (hid * up_pre * sig * (1.0 + gate_pre * (1.0 - sig))).astype(BF16)

        def product(q):
            columns = slice(q * part, (q + 1) * part)
            return dot(gate_grad, gate[:, columns]) + dot(up_grad, up[:, columns])

        emit(g, 1, product)

    over_groups(second)
    start_cross(1)
    start_home(0)
    start_side(1)

    def spread(g):
        active = act[0, g].astype(F32)
        parts = []
        for piece in (active[: group * 8], active[group * 8 :]):
            piece = piece.reshape(group, 1, 8, -1)
            parts.append(jnp.concatenate([piece, piece], axis=1).reshape(group * 16, -1))
        wide[g] = jnp.concatenate(parts, axis=0).T

    over_groups(spread)
    lane = iota((1, 2 * group * 16), 1)
    packed_lane = jnp.where(lane < group * 16, (lane >> 3) & 1, (lane & 15) >> 1)
    is_trained = trained_ref[0] == expert
    for i in range(1, trained_ref.shape[0]):
        is_trained = jnp.logical_or(is_trained, trained_ref[i] == expert)

    def weight_step(q, carry):
        keep = packed_lane == jnp.where(lane < group * 16, q // 4, q)

        def term(g):
            left = jnp.where(keep, wide[g], 0.0).astype(BF16)
            return dot(left, packed(1, g, q))

        if groups == 1:
            product = term(0)
        else:
            product = lax.fori_loop(
                1, groups, lambda g, c: c + term(g), term(0)
            )
        dgrad[:, eighth(q)] = jnp.where(is_trained, product, 0.0).astype(BF16)
        return carry

    def came_home(a):
        for k in order:
            view = rets[a].at[back(k)]
            remote(view, view, zs_sem.at[a, 0], zr_sem.at[a, back(k)], core_peer).wait_recv()
        for b, k, copy in zshare_copies:
            if b == a and k == 0:
                copy.wait()

    stores = []

    def weights_part():
        lax.fori_loop(0, 8, weight_step, 0)
        copy = pltpu.make_async_copy(dgrad, dgrad_hbm, out_sem.at[0])
        copy.start()
        stores.append(copy)

    def layer_part():
        came_home(0)
        combine(ids_ref, slots_ref, weights_ref, home, layer)
        copy = pltpu.make_async_copy(layer, layer_hbm, out_sem.at[1])
        copy.start()
        stores.append(copy)

    start_home(1, [weights_part, layer_part])
    came_home(1)
    for copy in cross_copies:
        copy.wait_send()
    for copy in yshare_copies.values():
        copy.wait_send()
    for a, k, copy in zshare_copies:
        if k != 0:
            copy.wait_send()
    for copy in stores:
        copy.wait()


def combine(ids_ref, slots_ref, weights_ref, packed, out_ref):
    experts = packed.shape[0]
    count, model = out_ref.shape
    part = model // 8
    rows = experts * 16
    lane = iota((1, 2 * rows), 1)
    base = (lax.rem(lane, rows) >> 4) * SLOTS
    is_main = lane < rows
    codes, factors = [], []
    for k in range(ids_ref.shape[0]):
        slot = slots_ref[k : k + 1, :]
        code = jnp.where(slot < SLOTS, ids_ref[k : k + 1, :] * SLOTS + slot, -1)
        codes.append(jnp.broadcast_to(code.astype(F32), (2 * rows, count)).T)
        if weights_ref is not None:
            factors.append(jnp.broadcast_to(weights_ref[k : k + 1, :], (128, count)).T)
    tail = packed[:, :, model // 2 :].reshape(rows, part)
    for q in range(8):
        held = jnp.where(is_main, (lane >> 3) & 1, (lane & 15) >> 1)
        hit = held == jnp.where(is_main, q // 4, q)
        want = jnp.where(is_main, base + (lane & 7), base + FULL + (lane & 1))
        want = jnp.where(hit, want, -2).astype(F32)
        b = q % 4
        main = packed[:, :, b * part : (b + 1) * part].reshape(rows, part)
        right = jnp.concatenate([main, tail], axis=0)
        result = None
        for k in range(len(codes)):
            term = dot(jnp.where(codes[k] == want, 1.0, 0.0).astype(BF16), right)
            if weights_ref is not None:
                term = term * jnp.concatenate([factors[k]] * (part // 128), axis=1)
            result = term if result is None else result + term
        out_ref[:, q * part : (q + 1) * part] = result.astype(BF16)


def combine_kernel(
    ids_ref,
    slots_ref,
    ret_ref,
    layer_hbm,
    dgrad_hbm,
    layer_out,
    grad_ref,
    dgrad_out,
    sems,
):
    copies = [
        pltpu.make_async_copy(layer_hbm, layer_out, sems.at[0]),
        pltpu.make_async_copy(dgrad_hbm, dgrad_out, sems.at[1]),
    ]
    for copy in copies:
        copy.start()
    combine(ids_ref, slots_ref, None, ret_ref, grad_ref)
    for copy in copies:
        copy.wait()


def local(
    n,
    tokens,
    expert_ids,
    slot_ids,
    route_weights,
    cotangent,
    gate_weight,
    up_weight,
    down_weight,
    trained,
):
    experts = n // SLICES
    count, model = tokens.shape
    hid = gate_weight.shape[1]
    packed = model * SLOTS // 16
    group = min(n, 16)
    groups = n // group
    ids, slots, weights = expert_ids.T, slot_ids.T, route_weights.T
    vmem = pl.BlockSpec(memory_space=pltpu.VMEM)
    anywhere = pl.BlockSpec(memory_space=pl.ANY)
    dma = pltpu.SemaphoreType.DMA
    returned, layer_rows, weight_rows = pl.pallas_call(
        functools.partial(exchange_kernel, n),
        out_shape=(
            jax.ShapeDtypeStruct((experts, 16, packed), BF16),
            jax.ShapeDtypeStruct((count, model), BF16),
            jax.ShapeDtypeStruct((hid, model), BF16),
        ),
        in_specs=[vmem] * 3 + [pl.BlockSpec(memory_space=pltpu.SMEM)] + [anywhere] * 5,
        out_specs=(anywhere, anywhere, anywhere),
        scratch_shapes=[
            pltpu.VMEM((count, model), BF16),
            pltpu.VMEM((count, model), BF16),
            pltpu.VMEM((hid, model), BF16),
            pltpu.VMEM((hid, model), BF16),
            pltpu.VMEM((hid, model), BF16),
            pltpu.VMEM((2, experts, 16, packed), BF16),
            pltpu.VMEM((2, n, 16, packed), BF16),
            pltpu.VMEM((2, group * 32, hid), F32),
            pltpu.VMEM((2, groups, group * 16, hid), F32),
            pltpu.VMEM((1, groups, group * 16, hid), BF16),
            pltpu.VMEM((groups, hid, group * 32), F32),
            pltpu.VMEM((2, 2, n // 2, 16, packed), BF16),
            pltpu.VMEM((2, n // 2, 16, packed), BF16),
            pltpu.VMEM((2, experts, 16, packed), BF16),
            pltpu.VMEM((2, experts, 16, packed), BF16),
            pltpu.VMEM((experts, 16, packed), BF16),
            pltpu.VMEM((count, model), BF16),
            pltpu.VMEM((hid, model), BF16),
            dma((5,)),
            dma((2, experts)),
            dma((2, experts)),
            dma((2, 2 * experts)),
            dma((2, n)),
            dma((2,)),
            dma((2, experts)),
            dma((2, experts)),
            dma((2, experts)),
            dma((2, experts)),
            dma((2, experts)),
            dma((2, experts)),
            dma((2,)),
        ],
        compiler_params=pltpu.CompilerParams(
            collective_id=0, has_side_effects=True, vmem_limit_bytes=62 * 2**20
        ),
        name="exchange",
    )(ids, slots, weights, trained, tokens, cotangent, gate_weight.T, up_weight.T, down_weight)

    return pl.pallas_call(
        combine_kernel,
        out_shape=(
            jax.ShapeDtypeStruct((count, model), BF16),
            jax.ShapeDtypeStruct((count, model), BF16),
            jax.ShapeDtypeStruct((hid, model), BF16),
        ),
        in_specs=[vmem, vmem, vmem, anywhere, anywhere],
        out_specs=(anywhere, vmem, anywhere),
        scratch_shapes=[dma((2,))],
        compiler_params=pltpu.CompilerParams(vmem_limit_bytes=24 * 2**20),
        name="combine",
    )(ids, slots, returned, layer_rows, weight_rows)


def solution(mesh):
    spread = P(("groups", "expert"), None)
    placed = (
        spread,
        spread,
        spread,
        spread,
        spread,
        P(None, "expert"),
        P(None, "expert"),
        P("expert", None),
        P("groups"),
    )
    return jax.shard_map(
        functools.partial(local, mesh.shape["expert"]),
        mesh=mesh,
        in_specs=placed,
        out_specs=(spread, spread, spread),
        check_vma=False,
    )
```

```python
import functools

import jax
import jax.numpy as jnp
from jax import lax
from jax.experimental import pallas as pl
from jax.experimental.pallas import tpu as pltpu
from jax.sharding import PartitionSpec as P

SLICES = 4
SLOTS = 10
FULL = 8
WINDOW = 2
MESH = pl.DeviceIdType.MESH
F32 = jnp.float32
BF16 = jnp.bfloat16


def iota(shape, dim):
    return lax.broadcasted_iota(jnp.int32, shape, dim)


def dot(a, b, ca=1, cb=0):
    return lax.dot_general(a, b, (((ca,), (cb,)), ((), ())), preferred_element_type=F32)


def fold(low, high, blocks, b, tail):
    width = low.shape[1]
    split = blocks * 8

    def pair(lo, hi):
        lo = lo.reshape(blocks, 1, 8, width)
        hi = hi.reshape(blocks, 1, 8, width)
        return jnp.concatenate([lo, hi], axis=1).reshape(blocks, 16, width)

    main = pair(low[:split], high[:split]).astype(BF16)
    rest = pair(low[split:], high[split:])
    mine = ((iota((1, 16, 1), 1) & 7) >> 1) == b
    return main, jnp.where(mine, rest, tail)


def unfold(total, blocks):
    split = blocks * 16
    width = total.shape[1]
    main = total[:split].reshape(blocks, 2, 8, width)
    main = (main[:, 0] + main[:, 1]).reshape(blocks * 8, width)
    rest = total[split:].reshape(blocks, 2, 8, width)
    rest = rest[:, 0] + rest[:, 1]
    even = (iota((1, 8, 1), 1) & 1) == 0
    first = jnp.sum(jnp.where(even, rest, 0.0), axis=1, keepdims=True)
    second = jnp.sum(jnp.where(even, 0.0, rest), axis=1, keepdims=True)
    rest = jnp.where(even, first, second).reshape(blocks * 8, width)
    return jnp.concatenate([main, rest], axis=0)


def exchange_kernel(
    n,
    ids_ref,
    slots_ref,
    weights_ref,
    trained_ref,
    tokens_hbm,
    cot_hbm,
    gate_hbm,
    up_hbm,
    down_hbm,
    ret_ref,
    layer_hbm,
    dgrad_hbm,
    tokens,
    cot,
    gate,
    up,
    down,
    send,
    recv,
    total,
    hidden,
    act,
    wide,
    shares,
    cross,
    ysend,
    yrecv,
    home,
    layer,
    dgrad,
    load_sem,
    z_sem,
    y_sem,
    c_sem,
    recv_sem,
    own_sem,
    cs_sem,
    cr_sem,
    ys_sem,
    yr_sem,
    zs_sem,
    zr_sem,
    out_sem,
):
    experts = n // SLICES
    model = tokens.shape[1]
    part = model // 8
    body = model // 2
    group = min(n, 16)
    groups = n // group
    me = lax.axis_index("expert")
    expert, low = me // 4, lax.rem(me, 4)
    core, side = lax.rem(me, 2), low // 2
    core_peer = me + 1 - 2 * core
    side_peer = me + 2 - 4 * side
    order = list(range(1, experts))
    homeward = order[1:] + order[:1] + [0]
    rets = (home, ret_ref)

    def other(k):
        if experts & (experts - 1) == 0:
            step, out = 1, 0
            for bit in range(experts.bit_length() - 1):
                have = lax.rem(expert // step, 2)
                out = out + step * (1 - have if k & step else have)
                step *= 2
            return out
        return lax.rem(expert + k, experts)

    def back(k):
        if experts & (experts - 1) == 0:
            return other(k)
        return lax.rem(expert + experts - k, experts)

    def remote(src, dst, ssem, rsem, dev):
        return pltpu.make_async_remote_copy(
            src_ref=src,
            dst_ref=dst,
            send_sem=ssem,
            recv_sem=rsem,
            device_id={"expert": dev},
            device_id_type=MESH,
        )

    loads = [
        pltpu.make_async_copy(s, d, load_sem.at[i])
        for i, (s, d) in enumerate(
            [
                (tokens_hbm, tokens),
                (cot_hbm, cot),
                (gate_hbm, gate),
                (up_hbm, up),
                (down_hbm, down),
            ]
        )
    ]
    for copy in loads:
        copy.start()

    barrier = pltpu.get_barrier_semaphore()
    for k in range(1, experts):
        pl.semaphore_signal(
            barrier, inc=1, device_id={"expert": other(k) * 4 + low}, device_id_type=MESH
        )
    for dev in (core_peer, side_peer):
        pl.semaphore_signal(barrier, inc=1, device_id={"expert": dev}, device_id_type=MESH)

    rows = experts * 16
    row = iota((rows, 1), 0)
    half = experts * 8
    want = jnp.where(
        row < half,
        (row >> 3) * SLOTS + (row & 7),
        ((row - half) >> 3) * SLOTS + FULL + (row & 1),
    )
    placer = jnp.zeros((rows, tokens.shape[0]), F32)
    factor = jnp.zeros((rows, 1), F32)
    for k in range(ids_ref.shape[0]):
        slot = slots_ref[k : k + 1, :]
        code = jnp.where(slot < SLOTS, ids_ref[k : k + 1, :] * SLOTS + slot, -1)
        hit = code == want
        placer = jnp.where(hit, 1.0, placer)
        factor = factor + jnp.sum(
            jnp.where(hit, weights_ref[k : k + 1, :], 0.0), axis=1, keepdims=True
        )
    placer = placer.astype(BF16)

    z_copies, y_copies, c_copies, own = {}, {}, {}, []
    steps = [(a, k) for a in (0, 1) for k in order]

    def start_z(a, k):
        target = other(k)
        copy = remote(
            send.at[a, target],
            recv.at[a, me],
            z_sem.at[a, k],
            recv_sem.at[a, me],
            target * 4 + low,
        )
        copy.start()
        z_copies[a, k] = copy

    for a, source in enumerate((tokens, cot)):
        loads[a].wait()
        tail = jnp.zeros((experts, 16, part), F32)
        for b in range(4):
            lo = dot(placer, source[:, b * part : (b + 1) * part])
            hi = dot(placer, source[:, (b + 4) * part : (b + 5) * part])
            if a == 1:
                lo, hi = lo * factor, hi * factor
            main, tail = fold(lo, hi, experts, b, tail)
            send[a, :, :, b * part : (b + 1) * part] = main
        send[a, :, :, body:] = tail.astype(BF16)
        if a == 0:
            pl.semaphore_wait(barrier, experts + 1)
            for pair in steps[:WINDOW]:
                start_z(*pair)
        mine = send.at[a, expert]
        for book, sem, dev in ((y_copies, y_sem, side_peer), (c_copies, c_sem, core_peer)):
            copy = remote(mine, recv.at[a, me], sem.at[a, 0], recv_sem.at[a, me], dev)
            copy.start()
            book[a, 0] = copy
        copy = pltpu.make_async_copy(mine, recv.at[a, me], own_sem.at[a])
        copy.start()
        own.append(copy)

    def arrived(a, j):
        view = recv.at[a, j]
        remote(view, view, z_sem.at[a, 0], recv_sem.at[a, j], core_peer).wait_recv()

    def pass_side(a, k):
        j = back(k) * 4 + low + 2 - 4 * side
        arrived(a, j)
        view = recv.at[a, j]
        copy = remote(view, view, c_sem.at[a, experts + k], recv_sem.at[a, j], core_peer)
        copy.start()
        c_copies[a, experts + k] = copy

    def pass_step(at):
        a, k = steps[at]
        j = back(k) * 4 + low
        arrived(a, j)
        if at + WINDOW < len(steps):
            start_z(*steps[at + WINDOW])
        view = recv.at[a, j]
        for book, sem, dev in ((y_copies, y_sem, side_peer), (c_copies, c_sem, core_peer)):
            copy = remote(view, view, sem.at[a, k], recv_sem.at[a, j], dev)
            copy.start()
            book[a, k] = copy

    def gathered(a):
        for k in [0] + order:
            for other_side in (0, 1):
                j = back(k) * 4 + 2 * (side if other_side == 0 else 1 - side) + 1 - core
                arrived(a, j)
        own[a].wait()

    trow = iota((2 * group * 16, 1), 0)
    packed_row = jnp.where(trow < group * 16, (trow >> 3) & 1, (trow & 15) >> 1)

    def eighth(q):
        return pl.ds(pl.multiple_of(q * part, 128), part)

    def packed(a, g, q):
        at = pl.ds(g * group, group)
        main = recv[a, at, :, pl.ds(pl.multiple_of(lax.rem(q, 4) * part, 128), part)]
        rest = recv[a, at, :, body:]
        both = jnp.concatenate([main, rest], axis=0)
        return both.reshape(2 * group * 16, part)

    def picked(q):
        return packed_row == jnp.where(trow < group * 16, q // 4, q)

    def over_groups(step):
        if groups == 1:
            step(0)
        else:
            lax.fori_loop(0, groups, lambda g, c: (step(g), c)[1], 0)

    def project(g, a, products):
        for i in range(len(products)):
            total[i] = jnp.zeros(total.shape[1:], F32)

        def step(q, carry):
            left = packed(a, g, q)
            keep = picked(q)
            for i, product in enumerate(products):
                total[i] += jnp.where(keep, product(left, q), 0.0)
            return carry

        lax.fori_loop(0, 8, step, 0)
        return [unfold(total[i], group) for i in range(len(products))]

    def emit(g, a, product):
        tail = jnp.zeros((group, 16, part), F32)

        def put(value, columns):
            value = value.reshape(group // 2, 2, 16, part)
            at = pl.ds(g * (group // 2), group // 2)
            for parity in (0, 1):
                shares[a, parity, at, :, columns] = value[:, parity]

        for b in range(4):
            main, tail = fold(product(b), product(b + 4), group, b, tail)
            put(main, slice(b * part, (b + 1) * part))
        put(tail.astype(BF16), slice(body, body + part))

    cross_copies, yshare_copies, zshare_copies = [], {}, []

    def start_cross(a):
        for k in homeward:
            e = other(k)
            copy = remote(
                shares.at[a, 1 - core, pl.ds(2 * e, 2)],
                cross.at[a, pl.ds(2 * e, 2)],
                cs_sem.at[a, e],
                cr_sem.at[a, e],
                core_peer,
            )
            copy.start()
            cross_copies.append(copy)

    def start_side(a):
        for k in homeward:
            e = other(k)
            view = cross.at[a, pl.ds(2 * e, 2)]
            remote(view, view, cs_sem.at[a, e], cr_sem.at[a, e], core_peer).wait_recv()
            at = 2 * e + 1 - side
            ysend[a, e] = (
                shares[a, core, at].astype(F32) + cross[a, at].astype(F32)
            ).astype(BF16)
            copy = remote(
                ysend.at[a, e], yrecv.at[a, e], ys_sem.at[a, e], yr_sem.at[a, e], side_peer
            )
            copy.start()
            yshare_copies[a, k] = copy

    def start_home(a, between=()):
        for turn, k in enumerate(homeward):
            e = other(k)
            view = yrecv.at[a, e]
            remote(view, view, ys_sem.at[a, e], yr_sem.at[a, e], side_peer).wait_recv()
            at = 2 * e + side
            send[a, e] = (
                (shares[a, core, at].astype(F32) + cross[a, at].astype(F32))
                + yrecv[a, e].astype(F32)
            ).astype(BF16)
            if k == 0:
                copy = pltpu.make_async_copy(send.at[a, e], rets[a].at[e], own_sem.at[a])
            else:
                copy = remote(
                    send.at[a, e],
                    rets[a].at[expert],
                    zs_sem.at[a, k],
                    zr_sem.at[a, expert],
                    e * 4 + low,
                )
            copy.start()
            zshare_copies.append((a, k, copy))
            if turn < len(between):
                between[turn]()

    last = len(order)
    for at in range(last):
        pass_step(at)
        pass_side(0, at)
    pass_step(last)
    pass_side(0, last)
    gathered(0)
    loads[2].wait()
    loads[3].wait()
    loads[4].wait()

    def first(g):
        gate_pre, up_pre = project(
            g,
            0,
            [
                lambda left, q: dot(left, gate[:, eighth(q)], 1, 1),
                lambda left, q: dot(left, up[:, eighth(q)], 1, 1),
            ],
        )
        hidden[0, g] = gate_pre
        hidden[1, g] = up_pre
        active = (gate_pre * jax.nn.sigmoid(gate_pre) * up_pre).astype(BF16)
        act[0, g] = active
        emit(g, 0, lambda q: dot(active, down[:, q * part : (q + 1) * part]))

    over_groups(first)
    start_cross(0)
    for at in range(last + 1, 2 * last):
        pass_side(1, at - last - 1)
        pass_step(at)
    pass_side(1, last - 1)
    pass_side(1, last)
    gathered(1)
    start_side(0)
    for copy in z_copies.values():
        copy.wait_send()
    for book in (y_copies, c_copies):
        for a in (0, 1):
            book[a, 0].wait_send()

    def second(g):
        (hid,) = project(g, 1, [lambda left, q: dot(left, down[:, eighth(q)], 1, 1)])
        gate_pre, up_pre = hidden[0, g], hidden[1, g]
        sig = jax.nn.sigmoid(gate_pre)
        up_grad = (hid * (gate_pre * sig)).astype(BF16)
        gate_grad = (hid * up_pre * sig * (1.0 + gate_pre * (1.0 - sig))).astype(BF16)

        def product(q):
            columns = slice(q * part, (q + 1) * part)
            return dot(gate_grad, gate[:, columns]) + dot(up_grad, up[:, columns])

        emit(g, 1, product)

    over_groups(second)
    start_cross(1)
    start_home(0, [lambda: None, lambda: start_side(1)])

    def spread(g):
        active = act[0, g].astype(F32)
        parts = []
        for piece in (active[: group * 8], active[group * 8 :]):
            piece = piece.reshape(group, 1, 8, -1)
            parts.append(jnp.concatenate([piece, piece], axis=1).reshape(group * 16, -1))
        wide[g] = jnp.concatenate(parts, axis=0).T

    over_groups(spread)
    lane = iota((1, 2 * group * 16), 1)
    packed_lane = jnp.where(lane < group * 16, (lane >> 3) & 1, (lane & 15) >> 1)
    is_trained = trained_ref[0] == expert
    for i in range(1, trained_ref.shape[0]):
        is_trained = jnp.logical_or(is_trained, trained_ref[i] == expert)

    def weight_step(q, carry):
        keep = packed_lane == jnp.where(lane < group * 16, q // 4, q)

        def term(g):
            left = jnp.where(keep, wide[g], 0.0).astype(BF16)
            return dot(left, packed(1, g, q))

        if groups == 1:
            product = term(0)
        else:
            product = lax.fori_loop(
                1, groups, lambda g, c: c + term(g), term(0)
            )
        dgrad[:, eighth(q)] = jnp.where(is_trained, product, 0.0).astype(BF16)
        return carry

    def came_home(a):
        for k in order:
            view = rets[a].at[back(k)]
            remote(view, view, zs_sem.at[a, 0], zr_sem.at[a, back(k)], core_peer).wait_recv()
        for b, k, copy in zshare_copies:
            if b == a and k == 0:
                copy.wait()

    stores = []

    def weights_part():
        lax.fori_loop(0, 8, weight_step, 0)
        copy = pltpu.make_async_copy(dgrad, dgrad_hbm, out_sem.at[0])
        copy.start()
        stores.append(copy)

    def layer_part():
        came_home(0)
        combine(ids_ref, slots_ref, weights_ref, home, layer)
        copy = pltpu.make_async_copy(layer, layer_hbm, out_sem.at[1])
        copy.start()
        stores.append(copy)

    start_home(1, [weights_part, layer_part])
    for book in (y_copies, c_copies):
        for (a, k), copy in book.items():
            if k != 0:
                copy.wait_send()
    for copy in cross_copies:
        copy.wait_send()
    for copy in yshare_copies.values():
        copy.wait_send()
    came_home(1)
    for a, k, copy in zshare_copies:
        if k != 0:
            copy.wait_send()
    for copy in stores:
        copy.wait()


def combine(ids_ref, slots_ref, weights_ref, packed, out_ref):
    experts = packed.shape[0]
    count, model = out_ref.shape
    part = model // 8
    rows = experts * 16
    lane = iota((1, 2 * rows), 1)
    base = (lax.rem(lane, rows) >> 4) * SLOTS
    is_main = lane < rows
    codes, factors = [], []
    for k in range(ids_ref.shape[0]):
        slot = slots_ref[k : k + 1, :]
        code = jnp.where(slot < SLOTS, ids_ref[k : k + 1, :] * SLOTS + slot, -1)
        codes.append(jnp.broadcast_to(code.astype(F32), (2 * rows, count)).T)
        if weights_ref is not None:
            factors.append(jnp.broadcast_to(weights_ref[k : k + 1, :], (128, count)).T)
    tail = packed[:, :, model // 2 :].reshape(rows, part)
    for q in range(8):
        held = jnp.where(is_main, (lane >> 3) & 1, (lane & 15) >> 1)
        hit = held == jnp.where(is_main, q // 4, q)
        want = jnp.where(is_main, base + (lane & 7), base + FULL + (lane & 1))
        want = jnp.where(hit, want, -2).astype(F32)
        b = q % 4
        main = packed[:, :, b * part : (b + 1) * part].reshape(rows, part)
        right = jnp.concatenate([main, tail], axis=0)
        result = None
        for k in range(len(codes)):
            term = dot(jnp.where(codes[k] == want, 1.0, 0.0).astype(BF16), right)
            if weights_ref is not None:
                term = term * jnp.concatenate([factors[k]] * (part // 128), axis=1)
            result = term if result is None else result + term
        out_ref[:, q * part : (q + 1) * part] = result.astype(BF16)


def combine_kernel(
    ids_ref,
    slots_ref,
    ret_hbm,
    layer_hbm,
    dgrad_hbm,
    layer_out,
    grad_ref,
    dgrad_out,
    ret,
    layer,
    dgrad,
    sems,
):
    pairs = [(ret_hbm, ret), (layer_hbm, layer), (dgrad_hbm, dgrad)]
    loads = [pltpu.make_async_copy(s, d, sems.at[i]) for i, (s, d) in enumerate(pairs)]
    for copy in loads:
        copy.start()
    stores = [
        pltpu.make_async_copy(layer, layer_out, sems.at[3]),
        pltpu.make_async_copy(dgrad, dgrad_out, sems.at[4]),
    ]
    for load, store in zip(loads[1:], stores):
        load.wait()
        store.start()
    loads[0].wait()
    combine(ids_ref, slots_ref, None, ret, grad_ref)
    for copy in stores:
        copy.wait()


def local(
    n,
    tokens,
    expert_ids,
    slot_ids,
    route_weights,
    cotangent,
    gate_weight,
    up_weight,
    down_weight,
    trained,
):
    experts = n // SLICES
    count, model = tokens.shape
    hid = gate_weight.shape[1]
    packed = model * SLOTS // 16
    group = min(n, 16)
    groups = n // group
    ids, slots, weights = expert_ids.T, slot_ids.T, route_weights.T
    vmem = pl.BlockSpec(memory_space=pltpu.VMEM)
    anywhere = pl.BlockSpec(memory_space=pl.ANY)
    dma = pltpu.SemaphoreType.DMA
    returned, layer_rows, weight_rows = pl.pallas_call(
        functools.partial(exchange_kernel, n),
        out_shape=(
            jax.ShapeDtypeStruct((experts, 16, packed), BF16),
            jax.ShapeDtypeStruct((count, model), BF16),
            jax.ShapeDtypeStruct((hid, model), BF16),
        ),
        in_specs=[vmem] * 3 + [pl.BlockSpec(memory_space=pltpu.SMEM)] + [anywhere] * 5,
        out_specs=(anywhere, anywhere, anywhere),
        scratch_shapes=[
            pltpu.VMEM((count, model), BF16),
            pltpu.VMEM((count, model), BF16),
            pltpu.VMEM((hid, model), BF16),
            pltpu.VMEM((hid, model), BF16),
            pltpu.VMEM((hid, model), BF16),
            pltpu.VMEM((2, experts, 16, packed), BF16),
            pltpu.VMEM((2, n, 16, packed), BF16),
            pltpu.VMEM((2, group * 32, hid), F32),
            pltpu.VMEM((2, groups, group * 16, hid), F32),
            pltpu.VMEM((1, groups, group * 16, hid), BF16),
            pltpu.VMEM((groups, hid, group * 32), F32),
            pltpu.VMEM((2, 2, n // 2, 16, packed), BF16),
            pltpu.VMEM((2, n // 2, 16, packed), BF16),
            pltpu.VMEM((2, experts, 16, packed), BF16),
            pltpu.VMEM((2, experts, 16, packed), BF16),
            pltpu.VMEM((experts, 16, packed), BF16),
            pltpu.VMEM((count, model), BF16),
            pltpu.VMEM((hid, model), BF16),
            dma((5,)),
            dma((2, experts)),
            dma((2, experts)),
            dma((2, 2 * experts)),
            dma((2, n)),
            dma((2,)),
            dma((2, experts)),
            dma((2, experts)),
            dma((2, experts)),
            dma((2, experts)),
            dma((2, experts)),
            dma((2, experts)),
            dma((2,)),
        ],
        compiler_params=pltpu.CompilerParams(
            collective_id=0, has_side_effects=True, vmem_limit_bytes=62 * 2**20
        ),
        name="exchange",
    )(ids, slots, weights, trained, tokens, cotangent, gate_weight.T, up_weight.T, down_weight)

    return pl.pallas_call(
        combine_kernel,
        out_shape=(
            jax.ShapeDtypeStruct((count, model), BF16),
            jax.ShapeDtypeStruct((count, model), BF16),
            jax.ShapeDtypeStruct((hid, model), BF16),
        ),
        in_specs=[vmem, vmem, anywhere, anywhere, anywhere],
        out_specs=(anywhere, vmem, anywhere),
        scratch_shapes=[
            pltpu.VMEM((experts, 16, packed), BF16),
            pltpu.VMEM((count, model), BF16),
            pltpu.VMEM((hid, model), BF16),
            dma((5,)),
        ],
        compiler_params=pltpu.CompilerParams(vmem_limit_bytes=62 * 2**20),
        name="combine",
    )(ids, slots, returned, layer_rows, weight_rows)


def solution(mesh):
    spread = P(("groups", "expert"), None)
    placed = (
        spread,
        spread,
        spread,
        spread,
        spread,
        P(None, "expert"),
        P(None, "expert"),
        P("expert", None),
        P("groups"),
    )
    return jax.shard_map(
        functools.partial(local, mesh.shape["expert"]),
        mesh=mesh,
        in_specs=placed,
        out_specs=(spread, spread, spread),
        check_vma=False,
    )
```

```python
import functools

import jax
import jax.numpy as jnp
from jax import lax
from jax.experimental import pallas as pl
from jax.experimental.pallas import tpu as pltpu
from jax.sharding import PartitionSpec as P

SLICES = 4
SLOTS = 10
FULL = 8
WINDOW = 2
MESH = pl.DeviceIdType.MESH
F32 = jnp.float32
BF16 = jnp.bfloat16


def iota(shape, dim):
    return lax.broadcasted_iota(jnp.int32, shape, dim)


def dot(a, b, ca=1, cb=0):
    return lax.dot_general(a, b, (((ca,), (cb,)), ((), ())), preferred_element_type=F32)


def fold(low, high, blocks, b, tail):
    width = low.shape[1]
    split = blocks * 8

    def pair(lo, hi):
        lo = lo.reshape(blocks, 1, 8, width)
        hi = hi.reshape(blocks, 1, 8, width)
        return jnp.concatenate([lo, hi], axis=1).reshape(blocks, 16, width)

    main = pair(low[:split], high[:split]).astype(BF16)
    rest = pair(low[split:], high[split:])
    mine = ((iota((1, 16, 1), 1) & 7) >> 1) == b
    return main, jnp.where(mine, rest, tail)


def unfold(total, blocks):
    split = blocks * 16
    width = total.shape[1]
    main = total[:split].reshape(blocks, 2, 8, width)
    main = (main[:, 0] + main[:, 1]).reshape(blocks * 8, width)
    rest = total[split:].reshape(blocks, 2, 8, width)
    rest = rest[:, 0] + rest[:, 1]
    even = (iota((1, 8, 1), 1) & 1) == 0
    first = jnp.sum(jnp.where(even, rest, 0.0), axis=1, keepdims=True)
    second = jnp.sum(jnp.where(even, 0.0, rest), axis=1, keepdims=True)
    rest = jnp.where(even, first, second).reshape(blocks * 8, width)
    return jnp.concatenate([main, rest], axis=0)


def exchange_kernel(
    n,
    ids_ref,
    slots_ref,
    weights_ref,
    trained_ref,
    tokens_hbm,
    cot_hbm,
    gate_hbm,
    up_hbm,
    down_hbm,
    ret_ref,
    layer_hbm,
    dgrad_hbm,
    tokens,
    cot,
    gate,
    up,
    down,
    send,
    recv,
    total,
    hidden,
    act,
    wide,
    shares,
    cross,
    ysend,
    yrecv,
    home,
    layer,
    dgrad,
    load_sem,
    z_sem,
    y_sem,
    c_sem,
    recv_sem,
    own_sem,
    cs_sem,
    cr_sem,
    ys_sem,
    yr_sem,
    zs_sem,
    zr_sem,
    out_sem,
):
    experts = n // SLICES
    model = tokens.shape[1]
    part = model // 8
    body = model // 2
    group = min(n, 16)
    groups = n // group
    me = lax.axis_index("expert")
    expert, low = me // 4, lax.rem(me, 4)
    core, side = lax.rem(me, 2), low // 2
    core_peer = me + 1 - 2 * core
    side_peer = me + 2 - 4 * side
    order = list(range(1, experts))
    homeward = order[1:] + order[:1] + [0]
    rets = (home, ret_ref)

    def other(k):
        if experts & (experts - 1) == 0:
            step, out = 1, 0
            for bit in range(experts.bit_length() - 1):
                have = lax.rem(expert // step, 2)
                out = out + step * (1 - have if k & step else have)
                step *= 2
            return out
        return lax.rem(expert + k, experts)

    def back(k):
        if experts & (experts - 1) == 0:
            return other(k)
        return lax.rem(expert + experts - k, experts)

    def remote(src, dst, ssem, rsem, dev):
        return pltpu.make_async_remote_copy(
            src_ref=src,
            dst_ref=dst,
            send_sem=ssem,
            recv_sem=rsem,
            device_id={"expert": dev},
            device_id_type=MESH,
        )

    loads = [
        pltpu.make_async_copy(s, d, load_sem.at[i])
        for i, (s, d) in enumerate(
            [
                (tokens_hbm, tokens),
                (cot_hbm, cot),
                (gate_hbm, gate),
                (up_hbm, up),
                (down_hbm, down),
            ]
        )
    ]
    for copy in loads:
        copy.start()

    barrier = pltpu.get_barrier_semaphore()
    for k in range(1, experts):
        pl.semaphore_signal(
            barrier, inc=1, device_id={"expert": other(k) * 4 + low}, device_id_type=MESH
        )
    for dev in (core_peer, side_peer):
        pl.semaphore_signal(barrier, inc=1, device_id={"expert": dev}, device_id_type=MESH)

    rows = experts * 16
    row = iota((rows, 1), 0)
    half = experts * 8
    want = jnp.where(
        row < half,
        (row >> 3) * SLOTS + (row & 7),
        ((row - half) >> 3) * SLOTS + FULL + (row & 1),
    )
    placer = jnp.zeros((rows, tokens.shape[0]), F32)
    factor = jnp.zeros((rows, 1), F32)
    for k in range(ids_ref.shape[0]):
        slot = slots_ref[k : k + 1, :]
        code = jnp.where(slot < SLOTS, ids_ref[k : k + 1, :] * SLOTS + slot, -1)
        hit = code == want
        placer = jnp.where(hit, 1.0, placer)
        factor = factor + jnp.sum(
            jnp.where(hit, weights_ref[k : k + 1, :], 0.0), axis=1, keepdims=True
        )
    placer = placer.astype(BF16)

    z_copies, y_copies, c_copies, own = {}, {}, {}, []
    steps = [(a, k) for a in (0, 1) for k in order]

    def start_z(a, k):
        target = other(k)
        copy = remote(
            send.at[a, target],
            recv.at[a, me],
            z_sem.at[a, k],
            recv_sem.at[a, me],
            target * 4 + low,
        )
        copy.start()
        z_copies[a, k] = copy

    for a, source in enumerate((tokens, cot)):
        loads[a].wait()
        tail = jnp.zeros((experts, 16, part), F32)
        for b in range(4):
            lo = dot(placer, source[:, b * part : (b + 1) * part])
            hi = dot(placer, source[:, (b + 4) * part : (b + 5) * part])
            if a == 1:
                lo, hi = lo * factor, hi * factor
            main, tail = fold(lo, hi, experts, b, tail)
            send[a, :, :, b * part : (b + 1) * part] = main
        send[a, :, :, body:] = tail.astype(BF16)
        if a == 0:
            pl.semaphore_wait(barrier, experts + 1)
            for pair in steps[:WINDOW]:
                start_z(*pair)
        mine = send.at[a, expert]
        for book, sem, dev in ((y_copies, y_sem, side_peer), (c_copies, c_sem, core_peer)):
            copy = remote(mine, recv.at[a, me], sem.at[a, 0], recv_sem.at[a, me], dev)
            copy.start()
            book[a, 0] = copy
        copy = pltpu.make_async_copy(mine, recv.at[a, me], own_sem.at[a])
        copy.start()
        own.append(copy)

    def arrived(a, j):
        view = recv.at[a, j]
        remote(view, view, z_sem.at[a, 0], recv_sem.at[a, j], core_peer).wait_recv()

    def pass_side(a, k):
        j = back(k) * 4 + low + 2 - 4 * side
        arrived(a, j)
        view = recv.at[a, j]
        copy = remote(view, view, c_sem.at[a, experts + k], recv_sem.at[a, j], core_peer)
        copy.start()
        c_copies[a, experts + k] = copy

    def pass_step(at):
        a, k = steps[at]
        j = back(k) * 4 + low
        arrived(a, j)
        if at + WINDOW < len(steps):
            start_z(*steps[at + WINDOW])
        view = recv.at[a, j]
        for book, sem, dev in ((y_copies, y_sem, side_peer), (c_copies, c_sem, core_peer)):
            copy = remote(view, view, sem.at[a, k], recv_sem.at[a, j], dev)
            copy.start()
            book[a, k] = copy

    def gathered(a):
        for k in [0] + order:
            for other_side in (0, 1):
                j = back(k) * 4 + 2 * (side if other_side == 0 else 1 - side) + 1 - core
                arrived(a, j)
        own[a].wait()

    trow = iota((2 * group * 16, 1), 0)
    packed_row = jnp.where(trow < group * 16, (trow >> 3) & 1, (trow & 15) >> 1)

    def eighth(q):
        return pl.ds(pl.multiple_of(q * part, 128), part)

    def packed(a, g, q):
        at = pl.ds(g * group, group)
        main = recv[a, at, :, pl.ds(pl.multiple_of(lax.rem(q, 4) * part, 128), part)]
        rest = recv[a, at, :, body:]
        both = jnp.concatenate([main, rest], axis=0)
        return both.reshape(2 * group * 16, part)

    def picked(q):
        return packed_row == jnp.where(trow < group * 16, q // 4, q)

    def over_groups(step):
        if groups == 1:
            step(0)
        else:
            lax.fori_loop(0, groups, lambda g, c: (step(g), c)[1], 0)

    def project(g, a, products):
        for i in range(len(products)):
            total[i] = jnp.zeros(total.shape[1:], F32)

        def step(q, carry):
            left = packed(a, g, q)
            keep = picked(q)
            for i, product in enumerate(products):
                total[i] += jnp.where(keep, product(left, q), 0.0)
            return carry

        lax.fori_loop(0, 8, step, 0)
        return [unfold(total[i], group) for i in range(len(products))]

    def emit(g, a, product):
        tail = jnp.zeros((group, 16, part), F32)

        def put(value, columns):
            value = value.reshape(group // 2, 2, 16, part)
            at = pl.ds(g * (group // 2), group // 2)
            for parity in (0, 1):
                shares[a, parity, at, :, columns] = value[:, parity]

        for b in range(4):
            main, tail = fold(product(b), product(b + 4), group, b, tail)
            put(main, slice(b * part, (b + 1) * part))
        put(tail.astype(BF16), slice(body, body + part))

    cross_copies, yshare_copies, zshare_copies = [], {}, []

    def start_cross(a):
        for k in homeward:
            e = other(k)
            copy = remote(
                shares.at[a, 1 - core, pl.ds(2 * e, 2)],
                cross.at[a, pl.ds(2 * e, 2)],
                cs_sem.at[a, e],
                cr_sem.at[a, e],
                core_peer,
            )
            copy.start()
            cross_copies.append(copy)

    def start_side(a):
        for k in homeward:
            e = other(k)
            view = cross.at[a, pl.ds(2 * e, 2)]
            remote(view, view, cs_sem.at[a, e], cr_sem.at[a, e], core_peer).wait_recv()
            at = 2 * e + 1 - side
            ysend[a, e] = (
                shares[a, core, at].astype(F32) + cross[a, at].astype(F32)
            ).astype(BF16)
            copy = remote(
                ysend.at[a, e], yrecv.at[a, e], ys_sem.at[a, e], yr_sem.at[a, e], side_peer
            )
            copy.start()
            yshare_copies[a, k] = copy

    def start_home(a, between=()):
        for turn, k in enumerate(homeward):
            e = other(k)
            view = yrecv.at[a, e]
            remote(view, view, ys_sem.at[a, e], yr_sem.at[a, e], side_peer).wait_recv()
            at = 2 * e + side
            send[a, e] = (
                (shares[a, core, at].astype(F32) + cross[a, at].astype(F32))
                + yrecv[a, e].astype(F32)
            ).astype(BF16)
            if k == 0:
                copy = pltpu.make_async_copy(send.at[a, e], rets[a].at[e], own_sem.at[a])
            else:
                copy = remote(
                    send.at[a, e],
                    rets[a].at[expert],
                    zs_sem.at[a, k],
                    zr_sem.at[a, expert],
                    e * 4 + low,
                )
            copy.start()
            zshare_copies.append((a, k, copy))
            if turn < len(between):
                between[turn]()

    last = len(order)
    for at in range(last):
        pass_step(at)
        pass_side(0, at)
    pass_step(last)
    pass_side(0, last)
    gathered(0)
    loads[2].wait()
    loads[3].wait()
    loads[4].wait()

    def first(g):
        gate_pre, up_pre = project(
            g,
            0,
            [
                lambda left, q: dot(left, gate[:, eighth(q)], 1, 1),
                lambda left, q: dot(left, up[:, eighth(q)], 1, 1),
            ],
        )
        hidden[0, g] = gate_pre
        hidden[1, g] = up_pre
        active = (gate_pre * jax.nn.sigmoid(gate_pre) * up_pre).astype(BF16)
        act[0, g] = active
        emit(g, 0, lambda q: dot(active, down[:, q * part : (q + 1) * part]))

    over_groups(first)
    start_cross(0)
    for at in range(last + 1, 2 * last):
        pass_side(1, at - last - 1)
        pass_step(at)
    pass_side(1, last - 1)
    pass_side(1, last)
    gathered(1)
    start_side(0)
    for copy in z_copies.values():
        copy.wait_send()
    for book in (y_copies, c_copies):
        for a in (0, 1):
            book[a, 0].wait_send()

    def second(g):
        (hid,) = project(g, 1, [lambda left, q: dot(left, down[:, eighth(q)], 1, 1)])
        gate_pre, up_pre = hidden[0, g], hidden[1, g]
        sig = jax.nn.sigmoid(gate_pre)
        up_grad = (hid * (gate_pre * sig)).astype(BF16)
        gate_grad = (hid * up_pre * sig * (1.0 + gate_pre * (1.0 - sig))).astype(BF16)

        def product(q):
            columns = slice(q * part, (q + 1) * part)
            return dot(gate_grad, gate[:, columns]) + dot(up_grad, up[:, columns])

        emit(g, 1, product)

    over_groups(second)
    start_cross(1)
    start_home(0, [lambda: None, lambda: start_side(1)])

    def spread(g):
        active = act[0, g].astype(F32)
        parts = []
        for piece in (active[: group * 8], active[group * 8 :]):
            piece = piece.reshape(group, 1, 8, -1)
            parts.append(jnp.concatenate([piece, piece], axis=1).reshape(group * 16, -1))
        wide[g] = jnp.concatenate(parts, axis=0).T

    over_groups(spread)
    lane = iota((1, 2 * group * 16), 1)
    packed_lane = jnp.where(lane < group * 16, (lane >> 3) & 1, (lane & 15) >> 1)
    is_trained = trained_ref[0] == expert
    for i in range(1, trained_ref.shape[0]):
        is_trained = jnp.logical_or(is_trained, trained_ref[i] == expert)

    def weight_step(q, carry):
        keep = packed_lane == jnp.where(lane < group * 16, q // 4, q)

        def term(g):
            left = jnp.where(keep, wide[g], 0.0).astype(BF16)
            return dot(left, packed(1, g, q))

        if groups == 1:
            product = term(0)
        else:
            product = lax.fori_loop(
                1, groups, lambda g, c: c + term(g), term(0)
            )
        dgrad[:, eighth(q)] = jnp.where(is_trained, product, 0.0).astype(BF16)
        return carry

    def came_home(a):
        for k in order:
            view = rets[a].at[back(k)]
            remote(view, view, zs_sem.at[a, 0], zr_sem.at[a, back(k)], core_peer).wait_recv()
        for b, k, copy in zshare_copies:
            if b == a and k == 0:
                copy.wait()

    stores = []

    def weights_part():
        lax.fori_loop(0, 8, weight_step, 0)
        copy = pltpu.make_async_copy(dgrad, dgrad_hbm, out_sem.at[0])
        copy.start()
        stores.append(copy)

    def layer_part():
        came_home(0)
        combine(ids_ref, slots_ref, weights_ref, home, layer)
        copy = pltpu.make_async_copy(layer, layer_hbm, out_sem.at[1])
        copy.start()
        stores.append(copy)

    start_home(1, [weights_part, layer_part])
    for book in (y_copies, c_copies):
        for (a, k), copy in book.items():
            if k != 0:
                copy.wait_send()
    for copy in cross_copies:
        copy.wait_send()
    for copy in yshare_copies.values():
        copy.wait_send()
    came_home(1)
    for a, k, copy in zshare_copies:
        if k != 0:
            copy.wait_send()
    for copy in stores:
        copy.wait()


def combine(ids_ref, slots_ref, weights_ref, packed, out_ref, after=None):
    experts = packed.shape[0]
    count, model = out_ref.shape
    part = model // 8
    rows = experts * 16
    lane = iota((1, 2 * rows), 1)
    base = (lax.rem(lane, rows) >> 4) * SLOTS
    is_main = lane < rows
    codes, factors = [], []
    for k in range(ids_ref.shape[0]):
        slot = slots_ref[k : k + 1, :]
        code = jnp.where(slot < SLOTS, ids_ref[k : k + 1, :] * SLOTS + slot, -1)
        codes.append(jnp.broadcast_to(code.astype(F32), (2 * rows, count)).T)
        if weights_ref is not None:
            factors.append(jnp.broadcast_to(weights_ref[k : k + 1, :], (128, count)).T)
    tail = packed[:, :, model // 2 :].reshape(rows, part)
    for q in range(8):
        held = jnp.where(is_main, (lane >> 3) & 1, (lane & 15) >> 1)
        hit = held == jnp.where(is_main, q // 4, q)
        want = jnp.where(is_main, base + (lane & 7), base + FULL + (lane & 1))
        want = jnp.where(hit, want, -2).astype(F32)
        b = q % 4
        main = packed[:, :, b * part : (b + 1) * part].reshape(rows, part)
        right = jnp.concatenate([main, tail], axis=0)
        result = None
        for k in range(len(codes)):
            term = dot(jnp.where(codes[k] == want, 1.0, 0.0).astype(BF16), right)
            if weights_ref is not None:
                term = term * jnp.concatenate([factors[k]] * (part // 128), axis=1)
            result = term if result is None else result + term
        out_ref[:, q * part : (q + 1) * part] = result.astype(BF16)
        if after is not None:
            after(q)


def combine_kernel(
    ids_ref,
    slots_ref,
    ret_hbm,
    layer_hbm,
    dgrad_hbm,
    layer_out,
    grad_out,
    dgrad_out,
    ret,
    layer,
    dgrad,
    grad,
    sems,
):
    pairs = [(ret_hbm, ret), (layer_hbm, layer), (dgrad_hbm, dgrad)]
    loads = [pltpu.make_async_copy(s, d, sems.at[i]) for i, (s, d) in enumerate(pairs)]
    for copy in loads:
        copy.start()
    stores = [
        pltpu.make_async_copy(layer, layer_out, sems.at[3]),
        pltpu.make_async_copy(dgrad, dgrad_out, sems.at[4]),
    ]
    part = grad.shape[1] // 8

    def after(q):
        if q < 2:
            loads[q + 1].wait()
            stores[q].start()
        at = slice(q * part, (q + 1) * part)
        copy = pltpu.make_async_copy(grad.at[:, at], grad_out.at[:, at], sems.at[5 + q])
        copy.start()
        stores.append(copy)

    loads[0].wait()
    combine(ids_ref, slots_ref, None, ret, grad, after)
    for copy in stores:
        copy.wait()


def local(
    n,
    tokens,
    expert_ids,
    slot_ids,
    route_weights,
    cotangent,
    gate_weight,
    up_weight,
    down_weight,
    trained,
):
    experts = n // SLICES
    count, model = tokens.shape
    hid = gate_weight.shape[1]
    packed = model * SLOTS // 16
    group = min(n, 16)
    groups = n // group
    ids, slots, weights = expert_ids.T, slot_ids.T, route_weights.T
    vmem = pl.BlockSpec(memory_space=pltpu.VMEM)
    anywhere = pl.BlockSpec(memory_space=pl.ANY)
    dma = pltpu.SemaphoreType.DMA
    returned, layer_rows, weight_rows = pl.pallas_call(
        functools.partial(exchange_kernel, n),
        out_shape=(
            jax.ShapeDtypeStruct((experts, 16, packed), BF16),
            jax.ShapeDtypeStruct((count, model), BF16),
            jax.ShapeDtypeStruct((hid, model), BF16),
        ),
        in_specs=[vmem] * 3 + [pl.BlockSpec(memory_space=pltpu.SMEM)] + [anywhere] * 5,
        out_specs=(anywhere, anywhere, anywhere),
        scratch_shapes=[
            pltpu.VMEM((count, model), BF16),
            pltpu.VMEM((count, model), BF16),
            pltpu.VMEM((hid, model), BF16),
            pltpu.VMEM((hid, model), BF16),
            pltpu.VMEM((hid, model), BF16),
            pltpu.VMEM((2, experts, 16, packed), BF16),
            pltpu.VMEM((2, n, 16, packed), BF16),
            pltpu.VMEM((2, group * 32, hid), F32),
            pltpu.VMEM((2, groups, group * 16, hid), F32),
            pltpu.VMEM((1, groups, group * 16, hid), BF16),
            pltpu.VMEM((groups, hid, group * 32), F32),
            pltpu.VMEM((2, 2, n // 2, 16, packed), BF16),
            pltpu.VMEM((2, n // 2, 16, packed), BF16),
            pltpu.VMEM((2, experts, 16, packed), BF16),
            pltpu.VMEM((2, experts, 16, packed), BF16),
            pltpu.VMEM((experts, 16, packed), BF16),
            pltpu.VMEM((count, model), BF16),
            pltpu.VMEM((hid, model), BF16),
            dma((5,)),
            dma((2, experts)),
            dma((2, experts)),
            dma((2, 2 * experts)),
            dma((2, n)),
            dma((2,)),
            dma((2, experts)),
            dma((2, experts)),
            dma((2, experts)),
            dma((2, experts)),
            dma((2, experts)),
            dma((2, experts)),
            dma((2,)),
        ],
        compiler_params=pltpu.CompilerParams(
            collective_id=0, has_side_effects=True, vmem_limit_bytes=62 * 2**20
        ),
        name="exchange",
    )(ids, slots, weights, trained, tokens, cotangent, gate_weight.T, up_weight.T, down_weight)

    return pl.pallas_call(
        combine_kernel,
        out_shape=(
            jax.ShapeDtypeStruct((count, model), BF16),
            jax.ShapeDtypeStruct((count, model), BF16),
            jax.ShapeDtypeStruct((hid, model), BF16),
        ),
        in_specs=[vmem, vmem, anywhere, anywhere, anywhere],
        out_specs=(anywhere, anywhere, anywhere),
        scratch_shapes=[
            pltpu.VMEM((experts, 16, packed), BF16),
            pltpu.VMEM((count, model), BF16),
            pltpu.VMEM((hid, model), BF16),
            pltpu.VMEM((count, model), BF16),
            dma((13,)),
        ],
        compiler_params=pltpu.CompilerParams(vmem_limit_bytes=62 * 2**20),
        name="combine",
    )(ids, slots, returned, layer_rows, weight_rows)


def solution(mesh):
    spread = P(("groups", "expert"), None)
    placed = (
        spread,
        spread,
        spread,
        spread,
        spread,
        P(None, "expert"),
        P(None, "expert"),
        P("expert", None),
        P("groups"),
    )
    return jax.shard_map(
        functools.partial(local, mesh.shape["expert"]),
        mesh=mesh,
        in_specs=placed,
        out_specs=(spread, spread, spread),
        check_vma=False,
    )
```
